256 devices in a mesh: vv: 16 (over y, z_lo, core), oo: 16 (over x, z_hi).
Axes of the slice: x: 4, y: 4, z: 8 (z_hi: 4, z_lo: 2; z = z_hi * 2 + z_lo), core: 2. Of those that a mesh axis runs over, the one named last changes fastest.
Arguments:
- integrals: bfloat16 [16384, 256], P('vv', 'oo'), may hold values from -0.375 to 0.375
- amplitudes: bfloat16 [256, 16384], P('vv', 'oo'), may hold values from -6 to 6
- occ_energy: float32 [128], replicated, may hold values from -2 to -0.3
- vir_energy: float32 [128], replicated, may hold values from 0.1 to 3
Outputs:
- update: bfloat16 [16384, 16384], P('vv', 'oo')
The draws below stay inside these ranges and needn't reach their ends.
All inputs are finite; a program needn't handle non-finite values.
Results may differ from the reference program's by a relative error of at most 0.0085.
Values may be sent and summed in bfloat16 or wider, within the bound.
A program may use at most 64 MiB of HBM per device.

```python
import jax
import jax.numpy as jnp
from jax import lax

CD = 256
VW = 128
OW = 128


def block_scale(key, extent, split, smallest, high):
    factor_of, own = 1.0, jax.random.fold_in(key, 6)
    for dim, blocks in split:
        steps = jnp.exp(jax.random.uniform(jax.random.fold_in(own, dim), (blocks,), jnp.float32, smallest / len(split), high / len(split)))
        factor_of = factor_of * jnp.repeat(steps, extent[dim] // blocks).reshape([-1 if axis == dim else 1 for axis in range(len(extent))])
    return factor_of


def bell_draw(stream_key, shape, deviation, most, shards=(), held_as=jnp.bfloat16):
    entries = jax.random.normal(stream_key, shape, jnp.float32) * deviation
    if len(shards) > 0:
        entries = block_scale(stream_key, shape, shards, -0.22, 0.18) * entries
    return jnp.clip(entries, min=-most, max=most).astype(held_as)


def setup_inputs(seed: int = 0) -> dict:
    splits = jax.random.split(jax.random.key(seed), 5)
    integrals = bell_draw(splits[0], (VW * VW, CD), CD ** -0.5, 0.375, ((0, 16), (1, 16)))
    amplitudes = bell_draw(splits[1], (CD, OW * OW), 1.0, 6.0, ((0, 16), (1, 16)))
    occ_energy = jnp.clip(jax.random.uniform(splits[2], (OW,), jnp.float32, -2.0, -0.3), -2.0, -0.3)
    vir_energy = jnp.clip(jax.random.uniform(splits[3], (VW,), jnp.float32, 0.1, 3.0), 0.1, 3.0)
    return dict(integrals=integrals, amplitudes=amplitudes, occ_energy=occ_energy, vir_energy=vir_energy)


def reference(integrals, amplitudes, occ_energy, vir_energy):
    cube = integrals.reshape(VW, VW, CD)
    flipped = jnp.transpose(cube, (1, 0, 2))
    amp_mirror = jnp.transpose(amplitudes.reshape(CD, OW, OW), (0, 2, 1)).reshape(CD, OW * OW)
    pair_occ = (occ_energy[:, None] + occ_energy[None, :]).reshape(OW * OW)

    def one_row(index):
        direct = jnp.dot(cube[index], amplitudes, preferred_element_type=jnp.float32).astype(jnp.bfloat16)
        mirror = jnp.dot(flipped[index], amp_mirror, preferred_element_type=jnp.float32).astype(jnp.bfloat16)
        denom = pair_occ[None, :] - vir_energy[index] - vir_energy[:, None]
        total = direct.astype(jnp.float32) + mirror.astype(jnp.float32)
        return (total / denom).astype(jnp.bfloat16)

    rows = lax.map(one_row, jnp.arange(VW, dtype=jnp.int32))
    return rows.reshape(VW * VW, OW * OW)
```

```python
import functools

import jax
import jax.numpy as jnp
from jax import lax
from jax.experimental import pallas as pl
from jax.experimental.pallas import tpu as pltpu
from jax.sharding import PartitionSpec as P

MESH = pl.DeviceIdType.MESH
GROUP = 16
CDS = 16
OWN = 8
ORB = 128
WIDE = OWN * ORB
CD = GROUP * CDS


def ring(at, step, size):
    return lax.rem(at + step, size)


def slot(kind, owner):
    return pl.ds(pl.multiple_of(kind * CD + owner * CDS, CDS), CDS)


def split_by_partner(chunk, turn, pieces):
    for j in range(OWN):
        turn[pl.ds(j, CDS, stride=OWN), :] = chunk[:, j * ORB : (j + 1) * ORB].astype(jnp.float32)
    pieces[...] = turn[...].T.reshape(GROUP, OWN, ORB)


def join_from_partners(pieces, turn, chunk):
    rows = [pieces[p] for p in range(GROUP)]
    group = lax.broadcasted_iota(jnp.int32, (OWN, ORB), 1) // OWN
    for bit in (1, 2, 4, 8):
        high = (group & bit) != 0
        for low in range(GROUP):
            if low & bit == 0:
                first, second = rows[low], rows[low + bit]
                rows[low] = jnp.where(high, pltpu.roll(second, bit * OWN, 1), first)
                rows[low + bit] = jnp.where(high, second, pltpu.roll(first, ORB - bit * OWN, 1))
    for c in range(CDS):
        turn[c * OWN : (c + 1) * OWN, :] = rows[c]
    for i in range(OWN):
        chunk[:, i * ORB : (i + 1) * ORB] = turn[pl.ds(i, CDS, stride=OWN), :].astype(chunk.dtype)


def gather_kernel(
    int_in, amp_in, int_all, amp_all,
    int_out_pieces, int_in_pieces, amp_out_pieces, amp_in_pieces, turn,
    local_sem, pair_send, pair_recv, int_send, int_recv, amp_send, amp_recv,
):
    vv, oo = lax.axis_index("vv"), lax.axis_index("oo")
    y, z_lo, core = vv // 4, (vv // 2) % 2, vv % 2
    x, z_hi = oo // 4, oo % 4

    barrier = pltpu.get_barrier_semaphore()
    loads = [
        pltpu.make_async_copy(int_in, int_all.at[slot(0, oo)], local_sem.at[0]),
        pltpu.make_async_copy(amp_in, amp_all.at[slot(0, vv)], local_sem.at[1]),
    ]
    for load in loads:
        load.start()
    for k in range(1, GROUP):
        pl.semaphore_signal(barrier, inc=1, device_id=(ring(vv, k, GROUP), oo), device_id_type=MESH)
        pl.semaphore_signal(barrier, inc=1, device_id=(vv, ring(oo, k, GROUP)), device_id_type=MESH)
    for load in loads:
        load.wait()

    split_by_partner(int_all.at[slot(0, oo)], turn.at[0], int_out_pieces)
    split_by_partner(amp_all.at[slot(0, vv)], turn.at[1], amp_out_pieces)
    int_in_pieces[vv] = int_out_pieces[vv]
    amp_in_pieces[oo] = amp_out_pieces[oo]
    pl.semaphore_wait(barrier, 2 * (GROUP - 1))

    sent = []

    def send(src, dst, send_sem, recv_sem, device):
        copy = pltpu.make_async_remote_copy(
            src_ref=src, dst_ref=dst, send_sem=send_sem, recv_sem=recv_sem,
            device_id=device, device_id_type=MESH,
        )
        copy.start()
        sent.append(copy)

    used = {"int": 0, "amp": 0}

    def send_int(kind, owner, device):
        rows, n = slot(kind, owner), used["int"]
        used["int"] += 1
        send(int_all.at[rows], int_all.at[rows], int_send.at[n], int_recv.at[kind, owner], device)

    def send_amp(kind, owner, device):
        rows, n = slot(kind, owner), used["amp"]
        used["amp"] += 1
        send(amp_all.at[rows], amp_all.at[rows], amp_send.at[n], amp_recv.at[kind, owner], device)

    def wait_for(array, kind, owner, recv_sem):
        rows = array.at[slot(kind, owner)]
        pltpu.make_async_copy(rows, rows, recv_sem.at[kind, owner]).wait()

    x_peers = [ring(x, k, 4) for k in (1, 3, 2)]
    z_peers = [ring(z_hi, k, 4) for k in (1, 3, 2)]
    y_peers = [ring(y, k, 4) for k in (1, 3, 2)]

    def spread_int(kind):
        for z in z_peers:
            send_int(kind, oo, (vv, x * 4 + z))
        for other in x_peers:
            send_int(kind, oo, (vv, other * 4 + z_hi))

    def spread_amp(kind):
        send_amp(kind, vv, (vv + 2 - 4 * z_lo, oo))
        for other in y_peers:
            send_amp(kind, vv, (other * 4 + z_lo * 2 + core, oo))
        send_amp(kind, vv, (vv + 1 - 2 * core, oo))

    spread_int(0)
    spread_amp(0)
    for k in range(1, GROUP):
        v, o = ring(vv, k, GROUP), ring(oo, k, GROUP)
        send(int_out_pieces.at[v], int_in_pieces.at[vv], pair_send.at[0, k], pair_recv.at[0, vv], (v, oo))
        send(amp_out_pieces.at[o], amp_in_pieces.at[oo], pair_send.at[1, k], pair_recv.at[1, oo], (vv, o))
    for k in range(1, GROUP):
        v = ring(vv, k, GROUP)
        pltpu.make_async_copy(int_in_pieces.at[v], int_in_pieces.at[v], pair_recv.at[0, v]).wait()
    join_from_partners(int_in_pieces, turn.at[0], int_all.at[slot(1, oo)])
    spread_int(1)
    for k in range(1, GROUP):
        o = ring(oo, k, GROUP)
        pltpu.make_async_copy(amp_in_pieces.at[o], amp_in_pieces.at[o], pair_recv.at[1, o]).wait()
    join_from_partners(amp_in_pieces, turn.at[1], amp_all.at[slot(1, vv)])
    spread_amp(1)

    neighbour = vv + 2 - 4 * z_lo
    sibling = vv + 1 - 2 * core
    for kind in range(2):
        for z in z_peers:
            wait_for(int_all, kind, x * 4 + z, int_recv)
            for other in x_peers:
                send_int(kind, x * 4 + z, (vv, other * 4 + z_hi))
        wait_for(amp_all, kind, neighbour, amp_recv)
        for other in y_peers:
            send_amp(kind, neighbour, (other * 4 + z_lo * 2 + core, oo))
        send_amp(kind, neighbour, (sibling, oo))
    for kind in range(2):
        for other in y_peers:
            for z in (z_lo, 1 - z_lo):
                owner = other * 4 + z * 2 + core
                wait_for(amp_all, kind, owner, amp_recv)
                send_amp(kind, owner, (sibling, oo))
    for kind in range(2):
        for far in range(8):
            wait_for(amp_all, kind, far * 2 + 1 - core, amp_recv)
        for other in x_peers:
            for z in range(4):
                wait_for(int_all, kind, other * 4 + z, int_recv)
    for copy in sent:
        copy.wait_send()


def gathered(integrals_t, amplitudes):
    whole = pltpu.VMEM((2 * CD, WIDE), jnp.bfloat16)
    pieces = pltpu.VMEM((GROUP, OWN, ORB), jnp.float32)
    return pl.pallas_call(
        gather_kernel,
        out_shape=(whole, whole),
        in_specs=[pl.BlockSpec(memory_space=pl.ANY)] * 2,
        out_specs=(pl.BlockSpec(memory_space=pltpu.VMEM),) * 2,
        scratch_shapes=[
            pieces, pieces, pieces, pieces,
            pltpu.VMEM((2, ORB, ORB), jnp.float32),
            pltpu.SemaphoreType.DMA((2,)),
            pltpu.SemaphoreType.DMA((2, GROUP)),
            pltpu.SemaphoreType.DMA((2, GROUP)),
            pltpu.SemaphoreType.DMA((30,)),
            pltpu.SemaphoreType.DMA((2, GROUP)),
            pltpu.SemaphoreType.DMA((30,)),
            pltpu.SemaphoreType.DMA((2, GROUP)),
        ],
        compiler_params=pltpu.CompilerParams(
            collective_id=0, has_side_effects=True, vmem_limit_bytes=16 << 20
        ),
        name="gather_pairs",
    )(integrals_t, amplitudes)


ROWS = 256


def ladder_kernel(int_ref, amp_ref, occ_ref, vir_ref, occ_mine, vir_mine, out_ref):
    step = pl.program_id(0)
    total = lax.dot_general(
        int_ref[...], amp_ref[...], (((0,), (0,)), ((), ())), preferred_element_type=jnp.float32
    )
    pieces = []
    for a in range(ROWS // ORB):
        vir_pair = vir_mine[step * (ROWS // ORB) + a] + vir_ref[...]
        for i in range(OWN):
            denom = (occ_mine[i] + occ_ref[...]) - vir_pair
            block = total[a * ORB : (a + 1) * ORB, i * ORB : (i + 1) * ORB] / denom
            out_ref[a * ORB : (a + 1) * ORB, i * ORB : (i + 1) * ORB] = block.astype(out_ref.dtype)


def ladder(int_all, amp_all, occ_energy, vir_energy, occ_mine, vir_mine):
    smem = pl.BlockSpec(memory_space=pltpu.SMEM)
    return pl.pallas_call(
        ladder_kernel,
        grid=(WIDE // ROWS,),
        out_shape=jax.ShapeDtypeStruct((WIDE, WIDE), jnp.bfloat16),
        in_specs=[
            pl.BlockSpec((2 * CD, ROWS), lambda s: (0, s)),
            pl.BlockSpec((2 * CD, WIDE), lambda s: (0, 0)),
            pl.BlockSpec((1, ORB), lambda s: (0, 0)),
            pl.BlockSpec((ORB, 1), lambda s: (0, 0)),
            smem,
            smem,
        ],
        out_specs=pl.BlockSpec((ROWS, WIDE), lambda s: (s, 0)),
        compiler_params=pltpu.CompilerParams(vmem_limit_bytes=32 << 20),
        name="ladder_sum",
    )(int_all, amp_all, occ_energy.reshape(1, ORB), vir_energy.reshape(ORB, 1), occ_mine, vir_mine)


def on_device(integrals, amplitudes, occ_energy, vir_energy):
    int_all, amp_all = gathered(integrals.T, amplitudes)
    occ_mine = lax.dynamic_slice_in_dim(occ_energy, lax.axis_index("oo") * OWN, OWN, 0)
    vir_mine = lax.dynamic_slice_in_dim(vir_energy, lax.axis_index("vv") * OWN, OWN, 0)
    return ladder(int_all, amp_all, occ_energy, vir_energy, occ_mine, vir_mine)


def solution(mesh):
    placed = (P("vv", "oo"), P("vv", "oo"), P(), P())
    return jax.shard_map(
        on_device, mesh=mesh, in_specs=placed, out_specs=P("vv", "oo"), check_vma=False
    )
```

```python
import jax
import jax.numpy as jnp
from jax import lax
from jax.experimental import pallas as pl
from jax.experimental.pallas import tpu as pltpu
from jax.sharding import PartitionSpec as P

MESH = pl.DeviceIdType.MESH
GROUP = 16
CDS = 16
OWN = 8
ORB = 128
WIDE = OWN * ORB
CD = GROUP * CDS
RING = 4


def around(at, step):
    return (at + step + RING) % RING


def slot(kind, owner):
    return pl.ds(pl.multiple_of(kind * CD + owner * CDS, CDS), CDS)


def split_by_partner(chunk, turn, pieces):
    for j in range(OWN):
        turn[pl.ds(j, CDS, stride=OWN), :] = chunk[:, j * ORB : (j + 1) * ORB].astype(jnp.float32)
    pieces[...] = turn[...].T.reshape(pieces.shape)


def join_from_partners(rows, turn, chunk):
    group = lax.broadcasted_iota(jnp.int32, (OWN, ORB), 1) // OWN
    for bit in (1, 2, 4, 8):
        high = (group & bit) != 0
        for low in range(GROUP):
            if low & bit == 0:
                first, second = rows[low], rows[low + bit]
                rows[low] = jnp.where(high, pltpu.roll(second, bit * OWN, 1), first)
                rows[low + bit] = jnp.where(high, second, pltpu.roll(first, ORB - bit * OWN, 1))
    for c in range(CDS):
        turn[c * OWN : (c + 1) * OWN, :] = rows[c]
    for i in range(OWN):
        chunk[:, i * ORB : (i + 1) * ORB] = turn[pl.ds(i, CDS, stride=OWN), :].astype(chunk.dtype)


def gather_kernel(
    int_in, amp_in, occ_in, vir_in, int_all, amp_all, inverse,
    int_cut, int_y, int_z, int_core, amp_cut, amp_x, amp_z, amp_pass, turn,
    occ_row, vir_row, occ_at, vir_at,
    local_sem, pair_send, pair_recv, int_send, int_recv, amp_send, amp_recv,
):
    vv, oo = lax.axis_index("vv"), lax.axis_index("oo")
    y, z_lo, core = vv // 4, (vv // 2) % 2, vv % 2
    x, z_hi = oo // 4, oo % 4

    def at_y(step):
        return (around(y, step) * 4 + z_lo * 2 + core, oo)

    def at_x(step):
        return (vv, around(x, step) * 4 + z_hi)

    def at_z(step):
        return (vv, x * 4 + around(z_hi, step))

    across = (y * 4 + (1 - z_lo) * 2 + core, oo)
    sibling = (y * 4 + z_lo * 2 + 1 - core, oo)

    barrier = pltpu.get_barrier_semaphore()
    greeted = [at_z(1), at_z(-1), at_y(2), at_x(2), at_y(1), at_y(-1), at_x(1), at_x(-1), across, sibling]
    for device in greeted:
        pl.semaphore_signal(barrier, inc=1, device_id=device, device_id_type=MESH)
    loads = [
        pltpu.make_async_copy(int_in, int_all.at[slot(0, oo)], local_sem.at[0]),
        pltpu.make_async_copy(amp_in, amp_all.at[slot(0, vv)], local_sem.at[1]),
        pltpu.make_async_copy(occ_in, occ_row, local_sem.at[2]),
        pltpu.make_async_copy(vir_in, vir_row, local_sem.at[3]),
        pltpu.make_async_copy(occ_in, occ_at, local_sem.at[4]),
        pltpu.make_async_copy(vir_in, vir_at, local_sem.at[5]),
    ]
    for load in loads:
        load.start()
    for load in loads:
        load.wait()

    split_by_partner(amp_all.at[slot(0, vv)], turn.at[1], amp_cut)
    split_by_partner(int_all.at[slot(0, oo)], turn.at[0], int_cut)
    pl.semaphore_wait(barrier, len(greeted))

    sent = []

    def send(src, dst, send_sem, recv_sem, device):
        copy = pltpu.make_async_remote_copy(
            src_ref=src, dst_ref=dst, send_sem=send_sem, recv_sem=recv_sem,
            device_id=device, device_id_type=MESH,
        )
        copy.start()
        sent.append(copy)

    used = {"int": 0, "amp": 0, "pair": 0}

    def next_of(which):
        used[which] += 1
        return used[which] - 1

    def send_int(kind, owner, device):
        rows = int_all.at[slot(kind, owner)]
        send(rows, rows, int_send.at[next_of("int")], int_recv.at[kind, owner], device)

    def send_amp(kind, owner, device):
        rows = amp_all.at[slot(kind, owner)]
        send(rows, rows, amp_send.at[next_of("amp")], amp_recv.at[kind, owner], device)

    def send_pair(src, dst, arrival, device):
        send(src, dst, pair_send.at[next_of("pair")], pair_recv.at[arrival], device)

    def got(ref, sem):
        pltpu.make_async_copy(ref, ref, sem).wait()

    def got_int(kind, owner):
        got(int_all.at[slot(kind, owner)], int_recv.at[kind, owner])

    def got_amp(kind, owner):
        got(amp_all.at[slot(kind, owner)], amp_recv.at[kind, owner])

    vir_column = jnp.broadcast_to(vir_row[...], (ORB, ORB)).T

    def invert(blocks):
        for a in blocks:
            vir_pair = vir_at[0, vv * OWN + a] + vir_column
            for i in range(OWN):
                denom = (occ_at[0, oo * OWN + i] + occ_row[...]) - vir_pair
                inverse[a * ORB : (a + 1) * ORB, i * ORB : (i + 1) * ORB] = 1.0 / denom

    for step in (2, 1, -1):
        send_pair(amp_cut.at[around(x, step)], amp_x.at[x], 0 + step % RING, at_x(step))
        send_pair(int_cut.at[around(y, step)], int_y.at[y], 4 + step % RING, at_y(step))
    amp_x[x] = amp_cut[x]
    int_y[y] = int_cut[y]

    def spread_int(kind):
        for step in (1, -1):
            send_int(kind, oo, at_z(step))
        for step in (1, -1):
            send_int(kind, oo, at_x(step))

    def spread_amp(kind):
        send_amp(kind, vv, across)
        for step in (1, -1):
            send_amp(kind, vv, at_y(step))
        send_amp(kind, vv, sibling)

    def owner_int(x_step, z_step):
        return around(x, x_step) * 4 + around(z_hi, z_step)

    def owner_amp(y_step, other):
        return around(y, y_step) * 4 + (1 - z_lo if other else z_lo) * 2 + core

    def from_z(kind):
        for step in (-1, 1):
            got_int(kind, owner_int(0, step))
            if step == (-1 if kind == 0 else 1):
                send_int(kind, owner_int(0, step), at_z(-step))
            for along in (1, -1):
                send_int(kind, owner_int(0, step), at_x(along))

    def from_across(kind):
        got_amp(kind, owner_amp(0, True))
        for step in (1, -1):
            send_amp(kind, owner_amp(0, True), at_y(step))
        send_amp(kind, owner_amp(0, True), sibling)

    def from_far_z(kind):
        got_int(kind, owner_int(0, 2))
        for along in (1, -1):
            send_int(kind, owner_int(0, 2), at_x(along))

    def from_x(kind, z_step):
        up = z_step % 2 == 0
        for along in (-1, 1):
            got_int(kind, owner_int(along, z_step))
            if along == (-1 if up else 1):
                send_int(kind, owner_int(along, z_step), at_x(-along))

    def from_y(kind, other):
        for step in (-1, 1):
            got_amp(kind, owner_amp(step, other))
            if step == (1 if other else -1):
                send_amp(kind, owner_amp(step, other), at_y(-step))
            send_amp(kind, owner_amp(step, other), sibling)

    def from_far_y(kind, other):
        got_amp(kind, owner_amp(2, other))
        send_amp(kind, owner_amp(2, other), sibling)

    spread_int(0)
    spread_amp(0)

    for step in (1, -1, 2):
        got(amp_x.at[around(x, step)], pair_recv.at[0 + (-step) % RING])
    send_pair(amp_x.at[:, around(z_hi, 2)], amp_pass, 8, at_z(1))
    for step in (1, -1):
        send_pair(amp_x.at[:, around(z_hi, step)], amp_z.at[:, z_hi], 8 + step % RING if step < 0 else 9, at_z(step))
    amp_z[:, z_hi] = amp_x[:, z_hi]

    for step in (1, -1, 2):
        got(int_y.at[around(y, step)], pair_recv.at[4 + (-step) % RING])
    send_pair(int_y.at[:, 1 - z_lo], int_z.at[:, z_lo], 12, across)
    int_z[:, z_lo] = int_y[:, z_lo]
    invert(range(0, 2))

    got(int_z.at[:, 1 - z_lo], pair_recv.at[12])
    send_pair(int_z.at[:, :, 1 - core], int_core.at[:, :, core], 13, sibling)
    int_core[:, :, core] = int_z[:, :, core]

    from_z(0)
    from_across(0)
    got(amp_pass, pair_recv.at[8])
    send_pair(amp_pass, amp_z.at[:, around(z_hi, -1)], 10, at_z(1))

    got(int_core.at[:, :, 1 - core], pair_recv.at[13])
    join_from_partners(
        [int_core[p // 4, (p // 2) % 2, p % 2] for p in range(GROUP)], turn.at[0], int_all.at[slot(1, oo)]
    )
    spread_int(1)
    from_x(0, 0)
    from_y(0, False)

    got(amp_z.at[:, around(z_hi, -1)], pair_recv.at[9])
    got(amp_z.at[:, around(z_hi, 1)], pair_recv.at[11])
    got(amp_z.at[:, around(z_hi, 2)], pair_recv.at[10])
    join_from_partners([amp_z[p // 4, p % 4] for p in range(GROUP)], turn.at[1], amp_all.at[slot(1, vv)])
    spread_amp(1)

    from_far_z(0)
    from_y(0, True)
    from_x(0, -1)
    from_x(0, 1)
    invert(range(2, 4))
    from_z(1)
    from_x(0, 2)
    from_across(1)
    from_far_y(0, False)
    from_far_y(0, True)
    from_x(1, 0)
    invert(range(4, 6))
    from_y(1, False)
    from_far_z(1)
    invert(range(6, 8))
    from_x(1, -1)
    from_x(1, 1)
    from_y(1, True)
    from_x(1, 2)
    from_far_y(1, False)
    from_far_y(1, True)
    for kind in range(2):
        for z_step in range(4):
            got_int(kind, owner_int(2, z_step))
        for far in range(8):
            got_amp(kind, far * 2 + 1 - core)
    for copy in sent:
        copy.wait_send()


def gathered(integrals_t, amplitudes, occ_row, vir_row):
    whole = pltpu.VMEM((2 * CD, WIDE), jnp.bfloat16)

    def pieces(*shape):
        return pltpu.VMEM((*shape, OWN, ORB), jnp.float32)

    def dma(*shape):
        return pltpu.SemaphoreType.DMA(shape)

    held = [pltpu.with_memory_space_constraint(a, pltpu.HBM) for a in (integrals_t, amplitudes, occ_row, vir_row)]
    return pl.pallas_call(
        gather_kernel,
        out_shape=(whole, whole, pltpu.VMEM((WIDE, WIDE), jnp.float32)),
        in_specs=[pl.BlockSpec(memory_space=pltpu.HBM)] * 4,
        out_specs=(pl.BlockSpec(memory_space=pltpu.VMEM),) * 3,
        scratch_shapes=[
            pieces(4, 2, 2), pieces(4, 2, 2), pieces(4, 2, 2), pieces(4, 2, 2),
            pieces(4, 4), pieces(4, 4), pieces(4, 4), pieces(4),
            pltpu.VMEM((2, ORB, ORB), jnp.float32),
            pltpu.VMEM((1, ORB), jnp.float32), pltpu.VMEM((1, ORB), jnp.float32),
            pltpu.SMEM((1, ORB), jnp.float32), pltpu.SMEM((1, ORB), jnp.float32),
            dma(6), dma(12), dma(14), dma(38), dma(2, GROUP), dma(38), dma(2, GROUP),
        ],
        compiler_params=pltpu.CompilerParams(
            collective_id=0, has_side_effects=True, vmem_limit_bytes=32 << 20
        ),
        name="gather_pairs",
    )(*held)


ROWS = 256


def ladder_kernel(int_ref, amp_ref, inverse, out_ref, made, sems):
    copies = []
    for s in range(WIDE // ROWS):
        rows = pl.ds(s * ROWS, ROWS)
        total = lax.dot_general(
            int_ref[:, s * ROWS : (s + 1) * ROWS], amp_ref[...], (((0,), (0,)), ((), ())),
            preferred_element_type=jnp.float32,
        )
        made[rows, :] = (total * inverse[rows, :]).astype(made.dtype)
        copies.append(pltpu.make_async_copy(made.at[rows], out_ref.at[rows], sems.at[s]))
        copies[-1].start()
    for copy in copies:
        copy.wait()


def ladder(int_all, amp_all, inverse):
    return pl.pallas_call(
        ladder_kernel,
        out_shape=jax.ShapeDtypeStruct((WIDE, WIDE), jnp.bfloat16),
        in_specs=[pl.BlockSpec(memory_space=pltpu.VMEM)] * 3,
        out_specs=pl.BlockSpec(memory_space=pl.ANY),
        scratch_shapes=[
            pltpu.VMEM((WIDE, WIDE), jnp.bfloat16), pltpu.SemaphoreType.DMA((WIDE // ROWS,)),
        ],
        compiler_params=pltpu.CompilerParams(vmem_limit_bytes=32 << 20),
        name="ladder_sum",
    )(int_all, amp_all, inverse)


def on_device(integrals, amplitudes, occ_energy, vir_energy):
    return ladder(
        *gathered(integrals.T, amplitudes, occ_energy.reshape(1, ORB), vir_energy.reshape(1, ORB))
    )


def solution(mesh):
    placed = (P("vv", "oo"), P("vv", "oo"), P(), P())
    return jax.shard_map(
        on_device, mesh=mesh, in_specs=placed, out_specs=P("vv", "oo"), check_vma=False
    )
```

```python
import jax
import jax.numpy as jnp
from jax import lax
from jax.experimental import pallas as pl
from jax.experimental.pallas import tpu as pltpu
from jax.sharding import PartitionSpec as P

MESH = pl.DeviceIdType.MESH
GROUP = 16
CDS = 16
OWN = 8
ORB = 128
WIDE = OWN * ORB
CD = GROUP * CDS
RING = 4


def around(at, step):
    return (at + step + RING) % RING


def slot(kind, owner):
    return pl.ds(pl.multiple_of(kind * CD + owner * CDS, CDS), CDS)


def split_by_partner(chunk, turn, pieces):
    for j in range(OWN):
        turn[pl.ds(j, CDS, stride=OWN), :] = chunk[:, j * ORB : (j + 1) * ORB].astype(jnp.float32)
    pieces[...] = turn[...].T.reshape(pieces.shape)


def join_from_partners(rows, turn, chunk):
    group = lax.broadcasted_iota(jnp.int32, (OWN, ORB), 1) // OWN
    for bit in (1, 2, 4, 8):
        high = (group & bit) != 0
        for low in range(GROUP):
            if low & bit == 0:
                first, second = rows[low], rows[low + bit]
                rows[low] = jnp.where(high, pltpu.roll(second, bit * OWN, 1), first)
                rows[low + bit] = jnp.where(high, second, pltpu.roll(first, ORB - bit * OWN, 1))
    for c in range(CDS):
        turn[c * OWN : (c + 1) * OWN, :] = rows[c]
    for i in range(OWN):
        chunk[:, i * ORB : (i + 1) * ORB] = turn[pl.ds(i, CDS, stride=OWN), :].astype(chunk.dtype)


def gather_kernel(
    int_in, amp_in, occ_in, vir_in, int_all, amp_all, inverse,
    int_cut, int_got, amp_cut, amp_x, amp_z, turn,
    occ_row, vir_row, occ_at, vir_at,
    local_sem, pair_send, pair_recv, int_send, int_recv, amp_send, amp_recv,
):
    vv, oo = lax.axis_index("vv"), lax.axis_index("oo")
    y, z_lo, core = vv // 4, (vv // 2) % 2, vv % 2
    x, z_hi = oo // 4, oo % 4

    def at_y(step):
        return (around(y, step) * 4 + z_lo * 2 + core, oo)

    def at_x(step):
        return (vv, around(x, step) * 4 + z_hi)

    def at_z(step):
        return (vv, x * 4 + around(z_hi, step))

    def at_chip(y_step, other):
        return (around(y, y_step) * 4 + (1 - z_lo if other else z_lo) * 2 + core, oo)

    def at_vv(step):
        return (lax.rem(vv + step, GROUP), oo)

    sibling = (y * 4 + z_lo * 2 + 1 - core, oo)
    near = (1, -1, 2)
    chips = [(step, other) for other in (False, True) for step in (0, *near) if step != 0 or other]

    barrier = pltpu.get_barrier_semaphore()
    greeted = [at_z(step) for step in near] + [at_x(step) for step in near] + [at_vv(step) for step in range(1, GROUP)]
    for device in greeted:
        pl.semaphore_signal(barrier, inc=1, device_id=device, device_id_type=MESH)
    loads = [
        pltpu.make_async_copy(int_in, int_all.at[slot(0, oo)], local_sem.at[0]),
        pltpu.make_async_copy(amp_in, amp_all.at[slot(0, vv)], local_sem.at[1]),
        pltpu.make_async_copy(occ_in, occ_row, local_sem.at[2]),
        pltpu.make_async_copy(vir_in, vir_row, local_sem.at[3]),
        pltpu.make_async_copy(occ_in, occ_at, local_sem.at[4]),
        pltpu.make_async_copy(vir_in, vir_at, local_sem.at[5]),
    ]
    for load in loads:
        load.start()
    for load in loads:
        load.wait()

    split_by_partner(amp_all.at[slot(0, vv)], turn.at[1], amp_cut)
    split_by_partner(int_all.at[slot(0, oo)], turn.at[0], int_cut)
    pl.semaphore_wait(barrier, len(greeted))

    sent = []

    def send(src, dst, send_sem, recv_sem, device):
        copy = pltpu.make_async_remote_copy(
            src_ref=src, dst_ref=dst, send_sem=send_sem, recv_sem=recv_sem,
            device_id=device, device_id_type=MESH,
        )
        copy.start()
        sent.append(copy)

    used = {"int": 0, "amp": 0, "pair": 0}

    def next_of(which):
        used[which] += 1
        return used[which] - 1

    def send_int(kind, owner, device):
        rows = int_all.at[slot(kind, owner)]
        send(rows, rows, int_send.at[next_of("int")], int_recv.at[kind, owner], device)

    def send_amp(kind, owner, device):
        rows = amp_all.at[slot(kind, owner)]
        send(rows, rows, amp_send.at[next_of("amp")], amp_recv.at[kind, owner], device)

    def send_pair(src, dst, arrival, device):
        send(src, dst, pair_send.at[next_of("pair")], pair_recv.at[arrival], device)

    def got(ref, sem):
        pltpu.make_async_copy(ref, ref, sem).wait()

    def got_int(kind, owner):
        got(int_all.at[slot(kind, owner)], int_recv.at[kind, owner])

    def got_amp(kind, owner):
        got(amp_all.at[slot(kind, owner)], amp_recv.at[kind, owner])

    vir_column = jnp.broadcast_to(vir_row[...], (ORB, ORB)).T

    def invert(blocks):
        for a in blocks:
            vir_pair = vir_at[0, vv * OWN + a] + vir_column
            for i in range(OWN):
                denom = (occ_at[0, oo * OWN + i] + occ_row[...]) - vir_pair
                inverse[a * ORB : (a + 1) * ORB, i * ORB : (i + 1) * ORB] = 1.0 / denom

    def spread_int(kind):
        for step in near:
            send_int(kind, oo, at_z(step))
        for step in near:
            send_int(kind, oo, at_x(step))

    def spread_amp(kind):
        for step, other in chips:
            send_amp(kind, vv, at_chip(step, other))
        send_amp(kind, vv, sibling)

    def owner_int(x_step, z_step):
        return around(x, x_step) * 4 + around(z_hi, z_step)

    def owner_amp(y_step, other):
        return around(y, y_step) * 4 + (1 - z_lo if other else z_lo) * 2 + core

    def onward_int(kind):
        for z_step in near:
            got_int(kind, owner_int(0, z_step))
            for step in near:
                send_int(kind, owner_int(0, z_step), at_x(step))

    def onward_amp(kind):
        for step, other in chips:
            got_amp(kind, owner_amp(step, other))
            send_amp(kind, owner_amp(step, other), sibling)

    for step in near:
        send_pair(amp_cut.at[around(x, step)], amp_x.at[x], step % RING, at_x(step))
    for step in range(1, GROUP):
        send_pair(int_cut.at[lax.rem(vv + step, GROUP)], int_got.at[vv], 8 + step, at_vv(step))
    amp_x[x] = amp_cut[x]
    int_got[vv] = int_cut[vv]
    spread_int(0)
    spread_amp(0)
    invert(range(0, 2))

    for step in near:
        got(amp_x.at[around(x, step)], pair_recv.at[-step % RING])
    for step in near:
        send_pair(amp_x.at[:, around(z_hi, step)], amp_z.at[:, z_hi], 4 + step % RING, at_z(step))
    amp_z[:, z_hi] = amp_x[:, z_hi]

    for step in range(1, GROUP):
        got(int_got.at[lax.rem(vv + GROUP - step, GROUP)], pair_recv.at[8 + step])
    join_from_partners([int_got[p] for p in range(GROUP)], turn.at[0], int_all.at[slot(1, oo)])
    spread_int(1)
    invert(range(2, 3))
    onward_int(0)

    for step in near:
        got(amp_z.at[:, around(z_hi, step)], pair_recv.at[4 + -step % RING])
    join_from_partners([amp_z[p // 4, p % 4] for p in range(GROUP)], turn.at[1], amp_all.at[slot(1, vv)])
    spread_amp(1)
    onward_amp(0)
    onward_int(1)
    invert(range(3, 8))
    onward_amp(1)
    for kind in range(2):
        for step in near:
            for z_step in range(4):
                got_int(kind, owner_int(step, z_step))
        for far in range(8):
            got_amp(kind, far * 2 + 1 - core)
    for copy in sent:
        copy.wait_send()


def gathered(integrals_t, amplitudes, occ_row, vir_row):
    whole = pltpu.VMEM((2 * CD, WIDE), jnp.bfloat16)

    def pieces(*shape):
        return pltpu.VMEM((*shape, OWN, ORB), jnp.float32)

    def dma(*shape):
        return pltpu.SemaphoreType.DMA(shape)

    held = [pltpu.with_memory_space_constraint(a, pltpu.HBM) for a in (integrals_t, amplitudes, occ_row, vir_row)]
    return pl.pallas_call(
        gather_kernel,
        out_shape=(whole, whole, pltpu.VMEM((WIDE, WIDE), jnp.float32)),
        in_specs=[pl.BlockSpec(memory_space=pltpu.HBM)] * 4,
        out_specs=(pl.BlockSpec(memory_space=pltpu.VMEM),) * 3,
        scratch_shapes=[
            pieces(GROUP), pieces(GROUP), pieces(4, 4), pieces(4, 4), pieces(4, 4),
            pltpu.VMEM((2, ORB, ORB), jnp.float32),
            pltpu.VMEM((1, ORB), jnp.float32), pltpu.VMEM((1, ORB), jnp.float32),
            pltpu.SMEM((1, ORB), jnp.float32), pltpu.SMEM((1, ORB), jnp.float32),
            dma(6), dma(21), dma(8 + GROUP), dma(30), dma(2, GROUP), dma(30), dma(2, GROUP),
        ],
        compiler_params=pltpu.CompilerParams(
            collective_id=0, has_side_effects=True, vmem_limit_bytes=32 << 20
        ),
        name="gather_pairs",
    )(*held)


ROWS = 256


def ladder_kernel(int_ref, amp_ref, inverse, out_ref, made, sems):
    copies = []
    for s in range(WIDE // ROWS):
        rows = pl.ds(s * ROWS, ROWS)
        total = lax.dot_general(
            int_ref[:, s * ROWS : (s + 1) * ROWS], amp_ref[...], (((0,), (0,)), ((), ())),
            preferred_element_type=jnp.float32,
        )
        made[rows, :] = (total * inverse[rows, :]).astype(made.dtype)
        copies.append(pltpu.make_async_copy(made.at[rows], out_ref.at[rows], sems.at[s]))
        copies[-1].start()
    for copy in copies:
        copy.wait()


def ladder(int_all, amp_all, inverse):
    return pl.pallas_call(
        ladder_kernel,
        out_shape=jax.ShapeDtypeStruct((WIDE, WIDE), jnp.bfloat16),
        in_specs=[pl.BlockSpec(memory_space=pltpu.VMEM)] * 3,
        out_specs=pl.BlockSpec(memory_space=pl.ANY),
        scratch_shapes=[
            pltpu.VMEM((WIDE, WIDE), jnp.bfloat16), pltpu.SemaphoreType.DMA((WIDE // ROWS,)),
        ],
        compiler_params=pltpu.CompilerParams(vmem_limit_bytes=32 << 20),
        name="ladder_sum",
    )(int_all, amp_all, inverse)


def on_device(integrals, amplitudes, occ_energy, vir_energy):
    return ladder(
        *gathered(integrals.T, amplitudes, occ_energy.reshape(1, ORB), vir_energy.reshape(1, ORB))
    )


def solution(mesh):
    placed = (P("vv", "oo"), P("vv", "oo"), P(), P())
    return jax.shard_map(
        on_device, mesh=mesh, in_specs=placed, out_specs=P("vv", "oo"), check_vma=False
    )
```

```python
import jax
import jax.numpy as jnp
from jax import lax
from jax.experimental import pallas as pl
from jax.experimental.pallas import tpu as pltpu
from jax.sharding import PartitionSpec as P

MESH = pl.DeviceIdType.MESH
GROUP = 16
CDS = 16
OWN = 8
ORB = 128
WIDE = OWN * ORB
CD = GROUP * CDS
RING = 4


def around(at, step):
    return (at + step + RING) % RING


def slot(kind, owner):
    return pl.ds(pl.multiple_of(kind * CD + owner * CDS, CDS), CDS)


def split_by_partner(chunk, turn):
    for j in range(OWN):
        turn[pl.ds(j, CDS, stride=OWN), :] = chunk[:, j * ORB : (j + 1) * ORB].astype(jnp.float32)
    turned = turn[...].T
    return [turned[p * OWN : (p + 1) * OWN] for p in range(GROUP)]


def swap_order(rows):
    return [rows[(p % RING) * RING + p // RING] for p in range(GROUP)]


def put_rows(rows, held):
    for q in range(RING):
        held[q] = jnp.concatenate(rows[q * RING : (q + 1) * RING], axis=0).astype(held.dtype)


def take_rows(held):
    blocks = [held[q].astype(jnp.float32) for q in range(RING)]
    return [blocks[p // RING][(p % RING) * OWN : (p % RING + 1) * OWN] for p in range(GROUP)]


def join_from_partners(rows, turn, chunk):
    group = lax.broadcasted_iota(jnp.int32, (OWN, ORB), 1) // OWN
    for bit in (1, 2, 4, 8):
        high = (group & bit) != 0
        for low in range(GROUP):
            if low & bit == 0:
                first, second = rows[low], rows[low + bit]
                rows[low] = jnp.where(high, pltpu.roll(second, bit * OWN, 1), first)
                rows[low + bit] = jnp.where(high, second, pltpu.roll(first, ORB - bit * OWN, 1))
    for c in range(CDS):
        turn[c * OWN : (c + 1) * OWN, :] = rows[c]
    for i in range(OWN):
        chunk[:, i * ORB : (i + 1) * ORB] = turn[pl.ds(i, CDS, stride=OWN), :].astype(chunk.dtype)


def gather_kernel(
    int_in, amp_in, occ_in, vir_in, int_all, amp_all, inverse,
    int_cut, int_got, amp_cut, amp_z, amp_cut_x, amp_x, turn,
    occ_row, vir_row, occ_at, vir_at,
    local_sem, pair_send, pair_recv, int_send, int_recv, amp_send, amp_recv,
):
    vv, oo = lax.axis_index("vv"), lax.axis_index("oo")
    y, z_lo, core = vv // 4, (vv // 2) % 2, vv % 2
    x, z_hi = oo // 4, oo % 4

    def at_y(step):
        return (around(y, step) * 4 + z_lo * 2 + core, oo)

    def at_x(step):
        return (vv, around(x, step) * 4 + z_hi)

    def at_z(step):
        return (vv, x * 4 + around(z_hi, step))

    def at_chip(y_step, other):
        return (around(y, y_step) * 4 + (1 - z_lo if other else z_lo) * 2 + core, oo)

    def at_vv(y_step, other, twin):
        return around(y, y_step) * 4 + (1 - z_lo if other else z_lo) * 2 + (1 - core if twin else core)

    sibling = (y * 4 + z_lo * 2 + 1 - core, oo)
    near, far_first = (1, -1, 2), (2, 1, -1)
    x_steps = ((1, -1), far_first)
    rows_of = [
        (y_step, other, twin)
        for y_step in (*far_first, 0) for other in (True, False) for twin in (True, False)
    ][:-1]
    chips = [(step, other) for other in (False, True) for step in (0, *near) if step != 0 or other]

    loads = [
        pltpu.make_async_copy(int_in, int_all.at[slot(0, oo)], local_sem.at[0]),
        pltpu.make_async_copy(amp_in, amp_all.at[slot(0, vv)], local_sem.at[1]),
        pltpu.make_async_copy(occ_in, occ_row, local_sem.at[2]),
        pltpu.make_async_copy(vir_in, vir_row, local_sem.at[3]),
        pltpu.make_async_copy(occ_in, occ_at, local_sem.at[4]),
        pltpu.make_async_copy(vir_in, vir_at, local_sem.at[5]),
    ]
    for load in loads:
        load.start()
    barrier = pltpu.get_barrier_semaphore()
    greeted = [at_z(step) for step in far_first] + [(at_vv(*steps), oo) for steps in rows_of] + [at_x(step) for step in far_first]
    for device in greeted:
        pl.semaphore_signal(barrier, inc=1, device_id=device, device_id_type=MESH)
    for load in loads[:2]:
        load.wait()

    put_rows(swap_order(split_by_partner(amp_all.at[slot(0, vv)], turn.at[1])), amp_cut)
    for p, row in enumerate(split_by_partner(int_all.at[slot(0, oo)], turn.at[0])):
        int_cut[p] = row
    pl.semaphore_wait(barrier, len(greeted))

    sent = []

    def send(src, dst, send_sem, recv_sem, device):
        copy = pltpu.make_async_remote_copy(
            src_ref=src, dst_ref=dst, send_sem=send_sem, recv_sem=recv_sem,
            device_id=device, device_id_type=MESH,
        )
        copy.start()
        sent.append(copy)

    used = {"int": 0, "amp": 0, "pair": 0}

    def next_of(which):
        used[which] += 1
        return used[which] - 1

    def send_int(kind, owner, device):
        rows = int_all.at[slot(kind, owner)]
        send(rows, rows, int_send.at[next_of("int")], int_recv.at[kind, owner], device)

    def send_amp(kind, owner, device):
        rows = amp_all.at[slot(kind, owner)]
        send(rows, rows, amp_send.at[next_of("amp")], amp_recv.at[kind, owner], device)

    def send_pair(src, dst, arrival, device):
        send(src, dst, pair_send.at[next_of("pair")], pair_recv.at[arrival], device)

    def got(ref, sem):
        pltpu.make_async_copy(ref, ref, sem).wait()

    def got_int(kind, owner):
        got(int_all.at[slot(kind, owner)], int_recv.at[kind, owner])

    def got_amp(kind, owner):
        got(amp_all.at[slot(kind, owner)], amp_recv.at[kind, owner])

    def spread_int(kind):
        for step in far_first:
            send_int(kind, oo, at_z(step))
        for step in (1, -1):
            send_int(kind, oo, at_x(step))

    def spread_amp(kind):
        for step, other in chips:
            send_amp(kind, vv, at_chip(step, other))
        send_amp(kind, vv, sibling)

    def owner_int(x_step, z_step):
        return around(x, x_step) * 4 + around(z_hi, z_step)

    def owner_amp(y_step, other):
        return around(y, y_step) * 4 + (1 - z_lo if other else z_lo) * 2 + core

    def onward_int(kind):
        for z_step in near:
            got_int(kind, owner_int(0, z_step))
            for step in x_steps[kind]:
                send_int(kind, owner_int(0, z_step), at_x(step))

    def relay_int(kind, z_step):
        first = -1 if z_step % 2 == 0 else 1
        got_int(kind, owner_int(first, z_step))
        send_int(kind, owner_int(first, z_step), at_x(-first))

    def onward_amp(kind):
        for step, other in chips:
            got_amp(kind, owner_amp(step, other))
            send_amp(kind, owner_amp(step, other), sibling)

    def spread_direct():
        send_amp(0, vv, at_chip(0, True))
        for step in far_first:
            send_amp(0, vv, at_chip(step, False))
        send_amp(0, vv, sibling)

    def onward_direct():
        got_amp(0, owner_amp(0, True))
        for step in far_first:
            send_amp(0, owner_amp(0, True), at_chip(step, False))
        send_amp(0, owner_amp(0, True), sibling)

    def pass_direct():
        for other in (False, True):
            for step in near:
                got_amp(0, owner_amp(step, other))
                send_amp(0, owner_amp(step, other), sibling)

    for step in far_first:
        send_pair(amp_cut.at[around(z_hi, step)], amp_z.at[z_hi], step % RING, at_z(step))
    for n, steps in enumerate(rows_of):
        partner = at_vv(*steps)
        send_pair(int_cut.at[partner], int_got.at[vv], 8 + n, (partner, oo))
    amp_z[z_hi] = amp_cut[z_hi]
    int_got[vv] = int_cut[vv]
    spread_int(0)
    spread_direct()
    for load in loads[2:]:
        load.wait()
    vir_column = jnp.broadcast_to(vir_row[...], (ORB, ORB)).T

    def invert(blocks):
        for a in blocks:
            vir_pair = vir_at[0, vv * OWN + a] + vir_column
            for i in range(OWN):
                denom = (occ_at[0, oo * OWN + i] + occ_row[...]) - vir_pair
                inverse[a * ORB : (a + 1) * ORB, i * ORB : (i + 1) * ORB] = 1.0 / denom

    invert(range(0, 2))

    for n, (y_step, other, twin) in enumerate(rows_of):
        back = y_step if y_step == 2 else -y_step
        got(int_got.at[at_vv(back, other, twin)], pair_recv.at[8 + n])

    for step in near:
        got(amp_z.at[around(z_hi, step)], pair_recv.at[-step % RING])
    put_rows(swap_order(take_rows(amp_z)), amp_cut_x)
    for step in far_first:
        send_pair(amp_cut_x.at[around(x, step)], amp_x.at[x], 4 + step % RING, at_x(step))
    amp_x[x] = amp_cut_x[x]
    join_from_partners([int_got[p] for p in range(GROUP)], turn.at[0], int_all.at[slot(1, oo)])
    spread_int(1)

    onward_direct()
    invert(range(2, 3))
    onward_int(0)
    relay_int(0, 0)

    for step in near:
        got(amp_x.at[around(x, step)], pair_recv.at[4 + -step % RING])
    join_from_partners(take_rows(amp_x), turn.at[1], amp_all.at[slot(1, vv)])
    spread_amp(1)
    relay_int(0, 1)
    relay_int(0, -1)
    pass_direct()
    relay_int(0, 2)
    relay_int(1, 0)
    onward_int(1)
    invert(range(3, 8))
    onward_amp(1)
    for kind in range(2):
        for z_step in (0, 1, -1, 2):
            for step in near:
                if (kind == 1 and z_step != 0) or step != (-1 if z_step % 2 == 0 else 1):
                    got_int(kind, owner_int(step, z_step))
        for far in range(8):
            got_amp(kind, far * 2 + 1 - core)
    for copy in sent:
        copy.wait_send()


def gathered(integrals_t, amplitudes, occ_row, vir_row):
    whole = pltpu.VMEM((2 * CD, WIDE), jnp.bfloat16)

    def pieces(*shape):
        return pltpu.VMEM((*shape, OWN, ORB), jnp.float32)

    blocks = pltpu.VMEM((RING, RING * OWN, ORB), jnp.bfloat16)

    def dma(*shape):
        return pltpu.SemaphoreType.DMA(shape)

    held = [pltpu.with_memory_space_constraint(a, pltpu.HBM) for a in (integrals_t, amplitudes, occ_row, vir_row)]
    return pl.pallas_call(
        gather_kernel,
        out_shape=(whole, whole, pltpu.VMEM((WIDE, WIDE), jnp.float32)),
        in_specs=[pl.BlockSpec(memory_space=pltpu.HBM)] * 4,
        out_specs=(pl.BlockSpec(memory_space=pltpu.VMEM),) * 3,
        scratch_shapes=[
            pieces(GROUP), pieces(GROUP), blocks, blocks, blocks, blocks,
            pltpu.VMEM((2, ORB, ORB), jnp.float32),
            pltpu.VMEM((1, ORB), jnp.float32), pltpu.VMEM((1, ORB), jnp.float32),
            pltpu.SMEM((1, ORB), jnp.float32), pltpu.SMEM((1, ORB), jnp.float32),
            dma(6), dma(21), dma(8 + GROUP), dma(30), dma(2, GROUP), dma(30), dma(2, GROUP),
        ],
        compiler_params=pltpu.CompilerParams(
            collective_id=0, has_side_effects=True, vmem_limit_bytes=32 << 20
        ),
        name="gather_pairs",
    )(*held)


ROWS = 256


def ladder_kernel(int_ref, amp_ref, inverse, out_ref, made, sems):
    copies = []
    for s in range(WIDE // ROWS):
        rows = pl.ds(s * ROWS, ROWS)
        total = lax.dot_general(
            int_ref[:, s * ROWS : (s + 1) * ROWS], amp_ref[...], (((0,), (0,)), ((), ())),
            preferred_element_type=jnp.float32,
        )
        made[rows, :] = (total * inverse[rows, :]).astype(made.dtype)
        copies.append(pltpu.make_async_copy(made.at[rows], out_ref.at[rows], sems.at[s]))
        copies[-1].start()
    for copy in copies:
        copy.wait()


def ladder(int_all, amp_all, inverse):
    return pl.pallas_call(
        ladder_kernel,
        out_shape=jax.ShapeDtypeStruct((WIDE, WIDE), jnp.bfloat16),
        in_specs=[pl.BlockSpec(memory_space=pltpu.VMEM)] * 3,
        out_specs=pl.BlockSpec(memory_space=pl.ANY),
        scratch_shapes=[
            pltpu.VMEM((WIDE, WIDE), jnp.bfloat16), pltpu.SemaphoreType.DMA((WIDE // ROWS,)),
        ],
        compiler_params=pltpu.CompilerParams(vmem_limit_bytes=32 << 20),
        name="ladder_sum",
    )(int_all, amp_all, inverse)


def on_device(integrals, amplitudes, occ_energy, vir_energy):
    return ladder(
        *gathered(integrals.T, amplitudes, occ_energy.reshape(1, ORB), vir_energy.reshape(1, ORB))
    )


def solution(mesh):
    placed = (P("vv", "oo"), P("vv", "oo"), P(), P())
    return jax.shard_map(
        on_device, mesh=mesh, in_specs=placed, out_specs=P("vv", "oo"), check_vma=False
    )
```

```python
import jax
import jax.numpy as jnp
from jax import lax
from jax.experimental import pallas as pl
from jax.experimental.pallas import tpu as pltpu
from jax.sharding import PartitionSpec as P

MESH = pl.DeviceIdType.MESH
GROUP = 16
CDS = 16
OWN = 8
ORB = 128
WIDE = OWN * ORB
CD = GROUP * CDS
RING = 4
ROWS = 256


def around(at, step):
    return (at + step + RING) % RING


def slot(kind, owner):
    return pl.ds(pl.multiple_of(kind * CD + owner * CDS, CDS), CDS)


def split_by_partner(chunk, turn):
    for j in range(OWN):
        turn[pl.ds(j, CDS, stride=OWN), :] = chunk[:, j * ORB : (j + 1) * ORB].astype(jnp.float32)
    turned = turn[...].T
    return [turned[p * OWN : (p + 1) * OWN] for p in range(GROUP)]


def swap_order(rows):
    return [rows[(p % RING) * RING + p // RING] for p in range(GROUP)]


def put_rows(rows, held):
    for q in range(RING):
        held[q] = jnp.concatenate(rows[q * RING : (q + 1) * RING], axis=0).astype(held.dtype)


def take_rows(held):
    blocks = [held[q].astype(jnp.float32) for q in range(RING)]
    return [blocks[p // RING][(p % RING) * OWN : (p % RING + 1) * OWN] for p in range(GROUP)]


def join_from_partners(rows, turn, chunk):
    group = lax.broadcasted_iota(jnp.int32, (OWN, ORB), 1) // OWN
    for bit in (1, 2, 4, 8):
        high = (group & bit) != 0
        for low in range(GROUP):
            if low & bit == 0:
                first, second = rows[low], rows[low + bit]
                rows[low] = jnp.where(high, pltpu.roll(second, bit * OWN, 1), first)
                rows[low + bit] = jnp.where(high, second, pltpu.roll(first, ORB - bit * OWN, 1))
    for c in range(CDS):
        turn[c * OWN : (c + 1) * OWN, :] = rows[c]
    for i in range(OWN):
        chunk[:, i * ORB : (i + 1) * ORB] = turn[pl.ds(i, CDS, stride=OWN), :].astype(chunk.dtype)


def gather_kernel(
    int_in, amp_in, occ_in, vir_in, int_all, amp_all, inverse, partial,
    int_cut, int_got, amp_cut, amp_z, amp_cut_x, amp_x, turn,
    occ_row, vir_row, occ_at, vir_at,
    local_sem, pair_send, pair_recv, int_send, int_recv, amp_send, amp_recv,
):
    vv, oo = lax.axis_index("vv"), lax.axis_index("oo")
    y, z_lo, core = vv // 4, (vv // 2) % 2, vv % 2
    x, z_hi = oo // 4, oo % 4

    def at_y(step):
        return (around(y, step) * 4 + z_lo * 2 + core, oo)

    def at_x(step):
        return (vv, around(x, step) * 4 + z_hi)

    def at_z(step):
        return (vv, x * 4 + around(z_hi, step))

    def at_chip(y_step, other):
        return (around(y, y_step) * 4 + (1 - z_lo if other else z_lo) * 2 + core, oo)

    def at_vv(y_step, other, twin):
        return around(y, y_step) * 4 + (1 - z_lo if other else z_lo) * 2 + (1 - core if twin else core)

    sibling = (y * 4 + z_lo * 2 + 1 - core, oo)
    near, far_first = (1, -1, 2), (2, 1, -1)
    x_steps = ((1, -1), far_first)
    rows_of = [
        (y_step, other, twin)
        for y_step in (*far_first, 0) for other in (True, False) for twin in (True, False)
    ][:-1]
    chips = [
        (1, False), (-1, False), (0, True), (2, False), (1, True), (-1, True), (2, True)
    ]

    barrier = pltpu.get_barrier_semaphore()
    greeted = [at_z(step) for step in far_first] + [(at_vv(*steps), oo) for steps in rows_of] + [at_x(step) for step in far_first]
    loads = [
        pltpu.make_async_copy(int_in, int_all.at[slot(0, oo)], local_sem.at[0]),
        pltpu.make_async_copy(amp_in, amp_all.at[slot(0, vv)], local_sem.at[1]),
        pltpu.make_async_copy(occ_in, occ_row, local_sem.at[2]),
        pltpu.make_async_copy(vir_in, vir_row, local_sem.at[3]),
        pltpu.make_async_copy(occ_in, occ_at, local_sem.at[4]),
        pltpu.make_async_copy(vir_in, vir_at, local_sem.at[5]),
    ]
    for n, device in enumerate(greeted):
        if n in (1, 2):
            loads[2 - n].start()
        pl.semaphore_signal(barrier, inc=1, device_id=device, device_id_type=MESH)
    for load in loads[2:]:
        load.start()

    loads[1].wait()
    put_rows(swap_order(split_by_partner(amp_all.at[slot(0, vv)], turn.at[1])), amp_cut)
    loads[0].wait()
    for p, row in enumerate(split_by_partner(int_all.at[slot(0, oo)], turn.at[0])):
        int_cut[p] = row
    pl.semaphore_wait(barrier, len(greeted))

    sent = []

    def send(src, dst, send_sem, recv_sem, device):
        copy = pltpu.make_async_remote_copy(
            src_ref=src, dst_ref=dst, send_sem=send_sem, recv_sem=recv_sem,
            device_id=device, device_id_type=MESH,
        )
        copy.start()
        sent.append(copy)

    used = {"int": 0, "amp": 0, "pair": 0}

    def next_of(which):
        used[which] += 1
        return used[which] - 1

    def send_int(kind, owner, device):
        rows = int_all.at[slot(kind, owner)]
        send(rows, rows, int_send.at[next_of("int")], int_recv.at[kind, owner], device)

    def send_amp(kind, owner, device):
        rows = amp_all.at[slot(kind, owner)]
        send(rows, rows, amp_send.at[next_of("amp")], amp_recv.at[kind, owner], device)

    def send_pair(src, dst, arrival, device):
        send(src, dst, pair_send.at[next_of("pair")], pair_recv.at[arrival], device)

    def got(ref, sem):
        pltpu.make_async_copy(ref, ref, sem).wait()

    def got_int(kind, owner):
        got(int_all.at[slot(kind, owner)], int_recv.at[kind, owner])

    def got_amp(kind, owner):
        got(amp_all.at[slot(kind, owner)], amp_recv.at[kind, owner])

    def spread_int(kind):
        for step in far_first:
            send_int(kind, oo, at_z(step))
        for step in (1, -1):
            send_int(kind, oo, at_x(step))

    def spread_amp(kind):
        for step, other in chips[::-1]:
            send_amp(kind, vv, at_chip(step, other))
        send_amp(kind, vv, sibling)

    def owner_int(x_step, z_step):
        return around(x, x_step) * 4 + around(z_hi, z_step)

    def owner_amp(y_step, other):
        return around(y, y_step) * 4 + (1 - z_lo if other else z_lo) * 2 + core

    def onward_int(kind, z_steps=near):
        for z_step in z_steps:
            got_int(kind, owner_int(0, z_step))
            for step in x_steps[kind]:
                send_int(kind, owner_int(0, z_step), at_x(step))

    def relay_int(kind, z_step):
        first = -1 if z_step % 2 == 0 else 1
        got_int(kind, owner_int(first, z_step))
        send_int(kind, owner_int(first, z_step), at_x(-first))

    def onward_amp(kind):
        for step, other in chips:
            got_amp(kind, owner_amp(step, other))
            send_amp(kind, owner_amp(step, other), sibling)

    def spread_direct():
        send_amp(0, vv, at_chip(0, True))
        for step in far_first:
            send_amp(0, vv, at_chip(step, False))
        send_amp(0, vv, sibling)

    def onward_direct():
        got_amp(0, owner_amp(0, True))
        for step in far_first:
            send_amp(0, owner_amp(0, True), at_chip(step, False))
        send_amp(0, owner_amp(0, True), sibling)

    def pass_direct():
        for other in (False, True):
            for step in near:
                got_amp(0, owner_amp(step, other))
                send_amp(0, owner_amp(step, other), sibling)

    for step in far_first:
        send_pair(amp_cut.at[around(z_hi, step)], amp_z.at[z_hi], step % RING, at_z(step))
    for n, steps in enumerate(rows_of):
        partner = at_vv(*steps)
        send_pair(int_cut.at[partner], int_got.at[vv], 8 + n, (partner, oo))
    amp_z[z_hi] = amp_cut[z_hi]
    int_got[vv] = int_cut[vv]
    spread_int(0)
    spread_direct()
    for load in loads[2:]:
        load.wait()
    vir_column = jnp.broadcast_to(vir_row[...], (ORB, ORB)).T

    def invert(blocks):
        for a in blocks:
            vir_pair = vir_at[0, vv * OWN + a] + vir_column
            for i in range(OWN):
                denom = (occ_at[0, oo * OWN + i] + occ_row[...]) - vir_pair
                inverse[a * ORB : (a + 1) * ORB, i * ORB : (i + 1) * ORB] = 1.0 / denom

    invert(range(0, 2))

    for n, (y_step, other, twin) in enumerate(rows_of):
        back = y_step if y_step == 2 else -y_step
        got(int_got.at[at_vv(back, other, twin)], pair_recv.at[8 + n])

    for step in near:
        got(amp_z.at[around(z_hi, step)], pair_recv.at[-step % RING])
    put_rows(swap_order(take_rows(amp_z)), amp_cut_x)
    for step in far_first:
        send_pair(amp_cut_x.at[around(x, step)], amp_x.at[x], 4 + step % RING, at_x(step))
    amp_x[x] = amp_cut_x[x]
    join_from_partners([int_got[p] for p in range(GROUP)], turn.at[0], int_all.at[slot(1, oo)])
    spread_int(1)

    onward_direct()
    invert(range(2, 3))
    onward_int(0)
    relay_int(0, 0)

    for step in near:
        got(amp_x.at[around(x, step)], pair_recv.at[4 + -step % RING])
    join_from_partners(take_rows(amp_x), turn.at[1], amp_all.at[slot(1, vv)])
    spread_amp(1)
    relay_int(0, 1)
    relay_int(0, -1)
    relay_int(1, 0)
    onward_int(1, (1, -1))
    relay_int(0, 2)
    onward_int(1, (2,))
    pass_direct()
    invert(range(3, 8))
    onward_amp(1)
    def finish(kind):
        for z_step in (0, 1, -1, 2):
            for step in near:
                if (kind == 1 and z_step != 0) or step != (-1 if z_step % 2 == 0 else 1):
                    got_int(kind, owner_int(step, z_step))
        for far in range(8):
            got_amp(kind, far * 2 + 1 - core)

    finish(0)
    for at in range(0, WIDE, ROWS):
        partial[at : at + ROWS] = lax.dot_general(
            int_all[:CD, at : at + ROWS], amp_all[:CD], (((0,), (0,)), ((), ())),
            preferred_element_type=jnp.float32,
        )
    finish(1)
    for copy in sent:
        copy.wait_send()


def gathered(integrals_t, amplitudes, occ_row, vir_row):
    whole = pltpu.VMEM((2 * CD, WIDE), jnp.bfloat16)

    square = pltpu.VMEM((WIDE, WIDE), jnp.float32)

    def pieces(*shape):
        return pltpu.VMEM((*shape, OWN, ORB), jnp.float32)

    blocks = pltpu.VMEM((RING, RING * OWN, ORB), jnp.bfloat16)

    def dma(*shape):
        return pltpu.SemaphoreType.DMA(shape)

    held = [pltpu.with_memory_space_constraint(a, pltpu.HBM) for a in (integrals_t, amplitudes, occ_row, vir_row)]
    return pl.pallas_call(
        gather_kernel,
        out_shape=(whole, whole, square, square),
        in_specs=[pl.BlockSpec(memory_space=pltpu.HBM)] * 4,
        out_specs=(pl.BlockSpec(memory_space=pltpu.VMEM),) * 4,
        scratch_shapes=[
            pieces(GROUP), pieces(GROUP), blocks, blocks, blocks, blocks,
            pltpu.VMEM((2, ORB, ORB), jnp.float32),
            pltpu.VMEM((1, ORB), jnp.float32), pltpu.VMEM((1, ORB), jnp.float32),
            pltpu.SMEM((1, ORB), jnp.float32), pltpu.SMEM((1, ORB), jnp.float32),
            dma(6), dma(21), dma(8 + GROUP), dma(30), dma(2, GROUP), dma(30), dma(2, GROUP),
        ],
        compiler_params=pltpu.CompilerParams(
            collective_id=0, has_side_effects=True, vmem_limit_bytes=32 << 20
        ),
        name="gather_pairs",
    )(*held)


def ladder_kernel(int_ref, amp_ref, inverse, partial, out_ref, made, sems):
    copies = []
    for s in range(WIDE // ROWS):
        rows = pl.ds(s * ROWS, ROWS)
        total = lax.dot_general(
            int_ref[CD:, s * ROWS : (s + 1) * ROWS], amp_ref[CD:], (((0,), (0,)), ((), ())),
            preferred_element_type=jnp.float32,
        )
        made[rows, :] = ((partial[rows, :] + total) * inverse[rows, :]).astype(made.dtype)
        copies.append(pltpu.make_async_copy(made.at[rows], out_ref.at[rows], sems.at[s]))
        copies[-1].start()
    for copy in copies:
        copy.wait()


def ladder(int_all, amp_all, inverse, partial):
    return pl.pallas_call(
        ladder_kernel,
        out_shape=jax.ShapeDtypeStruct((WIDE, WIDE), jnp.bfloat16),
        in_specs=[pl.BlockSpec(memory_space=pltpu.VMEM)] * 4,
        out_specs=pl.BlockSpec(memory_space=pl.ANY),
        scratch_shapes=[
            pltpu.VMEM((WIDE, WIDE), jnp.bfloat16), pltpu.SemaphoreType.DMA((WIDE // ROWS,)),
        ],
        compiler_params=pltpu.CompilerParams(vmem_limit_bytes=32 << 20),
        name="ladder_sum",
    )(int_all, amp_all, inverse, partial)


def on_device(integrals, amplitudes, occ_energy, vir_energy):
    return ladder(
        *gathered(integrals.T, amplitudes, occ_energy.reshape(1, ORB), vir_energy.reshape(1, ORB))
    )


def solution(mesh):
    placed = (P("vv", "oo"), P("vv", "oo"), P(), P())
    return jax.shard_map(
        on_device, mesh=mesh, in_specs=placed, out_specs=P("vv", "oo"), check_vma=False
    )
```

```python
import jax
import jax.numpy as jnp
from jax import lax
from jax.experimental import pallas as pl
from jax.experimental.pallas import tpu as pltpu
from jax.sharding import PartitionSpec as P

MESH = pl.DeviceIdType.MESH
GROUP = 16
CDS = 16
OWN = 8
ORB = 128
WIDE = OWN * ORB
CD = GROUP * CDS
RING = 4
ROWS = 256


def around(at, step):
    return (at + step + RING) % RING


def slot(kind, owner):
    return pl.ds(pl.multiple_of(kind * CD + owner * CDS, CDS), CDS)


def split_by_partner(chunk, turn):
    for j in range(OWN):
        turn[pl.ds(j, CDS, stride=OWN), :] = chunk[:, j * ORB : (j + 1) * ORB].astype(jnp.float32)
    turned = turn[...].T
    return [turned[p * OWN : (p + 1) * OWN] for p in range(GROUP)]


def swap_order(rows):
    return [rows[(p % RING) * RING + p // RING] for p in range(GROUP)]


def put_rows(rows, held):
    for q in range(RING):
        held[q] = jnp.concatenate(rows[q * RING : (q + 1) * RING], axis=0).astype(held.dtype)


def take_rows(held):
    blocks = [held[q].astype(jnp.float32) for q in range(RING)]
    return [blocks[p // RING][(p % RING) * OWN : (p % RING + 1) * OWN] for p in range(GROUP)]


def join_from_partners(rows, turn, chunk):
    group = lax.broadcasted_iota(jnp.int32, (OWN, ORB), 1) // OWN
    for bit in (1, 2, 4, 8):
        high = (group & bit) != 0
        for low in range(GROUP):
            if low & bit == 0:
                first, second = rows[low], rows[low + bit]
                rows[low] = jnp.where(high, pltpu.roll(second, bit * OWN, 1), first)
                rows[low + bit] = jnp.where(high, second, pltpu.roll(first, ORB - bit * OWN, 1))
    for c in range(CDS):
        turn[c * OWN : (c + 1) * OWN, :] = rows[c]
    for i in range(OWN):
        chunk[:, i * ORB : (i + 1) * ORB] = turn[pl.ds(i, CDS, stride=OWN), :].astype(chunk.dtype)


def gather_kernel(
    int_in, amp_in, occ_in, vir_in, int_all, amp_all, inverse, partial,
    int_cut, int_got, amp_cut, amp_z, amp_cut_x, amp_x, turn,
    occ_row, vir_row, occ_at, vir_at,
    local_sem, pair_send, pair_recv, int_send, int_recv, int_done, amp_send, amp_recv, amp_done,
):
    vv, oo = lax.axis_index("vv"), lax.axis_index("oo")
    y, z_lo, core = vv // 4, (vv // 2) % 2, vv % 2
    x, z_hi = oo // 4, oo % 4

    def at_y(step):
        return (around(y, step) * 4 + z_lo * 2 + core, oo)

    def at_x(step):
        return (vv, around(x, step) * 4 + z_hi)

    def at_z(step):
        return (vv, x * 4 + around(z_hi, step))

    def at_chip(y_step, other):
        return (around(y, y_step) * 4 + (1 - z_lo if other else z_lo) * 2 + core, oo)

    def at_vv(y_step, other, twin):
        return around(y, y_step) * 4 + (1 - z_lo if other else z_lo) * 2 + (1 - core if twin else core)

    sibling = (y * 4 + z_lo * 2 + 1 - core, oo)
    near, far_first = (1, -1, 2), (2, 1, -1)
    x_steps = ((1, -1), far_first)
    rows_of = [
        (y_step, other, twin)
        for y_step in (*far_first, 0) for other in (True, False) for twin in (True, False)
    ][:-1]
    chips = [
        (1, False), (-1, False), (0, True), (2, False), (1, True), (-1, True), (2, True)
    ]

    barrier = pltpu.get_barrier_semaphore()
    greeted = [at_z(step) for step in far_first] + [(at_vv(*steps), oo) for steps in rows_of] + [at_x(step) for step in far_first]
    loads = [
        pltpu.make_async_copy(int_in, int_all.at[slot(0, oo)], local_sem.at[0]),
        pltpu.make_async_copy(amp_in, amp_all.at[slot(0, vv)], local_sem.at[1]),
        pltpu.make_async_copy(occ_in, occ_row, local_sem.at[2]),
        pltpu.make_async_copy(vir_in, vir_row, local_sem.at[3]),
        pltpu.make_async_copy(occ_in, occ_at, local_sem.at[4]),
        pltpu.make_async_copy(vir_in, vir_at, local_sem.at[5]),
    ]
    for n, device in enumerate(greeted):
        if n in (1, 2):
            loads[2 - n].start()
        pl.semaphore_signal(barrier, inc=1, device_id=device, device_id_type=MESH)
    for load in loads[2:]:
        load.start()

    loads[1].wait()
    put_rows(swap_order(split_by_partner(amp_all.at[slot(0, vv)], turn.at[1])), amp_cut)
    loads[0].wait()
    for p, row in enumerate(split_by_partner(int_all.at[slot(0, oo)], turn.at[0])):
        int_cut[p] = row
    pl.semaphore_wait(barrier, len(greeted))

    def send(src, dst, send_sem, recv_sem, device):
        copy = pltpu.make_async_remote_copy(
            src_ref=src, dst_ref=dst, send_sem=send_sem, recv_sem=recv_sem,
            device_id=device, device_id_type=MESH,
        )
        copy.start()

    used = {"int": 0, "amp": 0}

    def send_int(kind, owner, device, last=False):
        rows = int_all.at[slot(kind, owner)]
        used["int"] += 1
        arrival = int_done.at[kind] if last else int_recv.at[kind, owner]
        send(rows, rows, int_send.at[0], arrival, device)

    def send_amp(kind, owner, device, last=False):
        rows = amp_all.at[slot(kind, owner)]
        used["amp"] += 1
        arrival = amp_done.at[kind] if last else amp_recv.at[kind, owner]
        send(rows, rows, amp_send.at[0], arrival, device)

    def send_pair(which, src, dst, arrival, device):
        send(src, dst, pair_send.at[which], pair_recv.at[arrival], device)

    def got(ref, sem):
        pltpu.make_async_copy(ref, ref, sem).wait()

    def got_int(kind, owner):
        got(int_all.at[slot(kind, owner)], int_recv.at[kind, owner])

    def got_amp(kind, owner):
        got(amp_all.at[slot(kind, owner)], amp_recv.at[kind, owner])

    def spread_int(kind):
        for step in far_first:
            send_int(kind, oo, at_z(step))
        for step in (1, -1):
            send_int(kind, oo, at_x(step), last=step == -1)

    def spread_amp(kind):
        for step, other in chips[::-1]:
            send_amp(kind, vv, at_chip(step, other))
        send_amp(kind, vv, sibling, last=True)

    def owner_int(x_step, z_step):
        return around(x, x_step) * 4 + around(z_hi, z_step)

    def owner_amp(y_step, other):
        return around(y, y_step) * 4 + (1 - z_lo if other else z_lo) * 2 + core

    def onward_int(kind, z_steps=near):
        for z_step in z_steps:
            got_int(kind, owner_int(0, z_step))
            for step in x_steps[kind]:
                last = kind == 1 or step != (1 if z_step % 2 == 0 else -1)
                send_int(kind, owner_int(0, z_step), at_x(step), last)

    def relay_int(kind, z_step):
        first = -1 if z_step % 2 == 0 else 1
        got_int(kind, owner_int(first, z_step))
        send_int(kind, owner_int(first, z_step), at_x(-first), last=True)

    def onward_amp(kind):
        for step, other in chips:
            got_amp(kind, owner_amp(step, other))
            send_amp(kind, owner_amp(step, other), sibling, last=True)

    def spread_direct():
        send_amp(0, vv, at_chip(0, True))
        for step in far_first:
            send_amp(0, vv, at_chip(step, False))
        send_amp(0, vv, sibling, last=True)

    def onward_direct():
        got_amp(0, owner_amp(0, True))
        for step in far_first:
            send_amp(0, owner_amp(0, True), at_chip(step, False))
        send_amp(0, owner_amp(0, True), sibling, last=True)

    def pass_direct():
        for other in (False, True):
            for step in near:
                got_amp(0, owner_amp(step, other))
                send_amp(0, owner_amp(step, other), sibling, last=True)

    for step in far_first:
        send_pair(0, amp_cut.at[around(z_hi, step)], amp_z.at[z_hi], step % RING, at_z(step))
    for steps in rows_of:
        partner = at_vv(*steps)
        send_pair(2, int_cut.at[partner], int_got.at[vv], 8, (partner, oo))
    amp_z[z_hi] = amp_cut[z_hi]
    int_got[vv] = int_cut[vv]
    spread_int(0)
    spread_direct()
    for load in loads[2:]:
        load.wait()
    vir_column = jnp.broadcast_to(vir_row[...], (ORB, ORB)).T

    def invert(blocks):
        for a in blocks:
            vir_pair = vir_at[0, vv * OWN + a] + vir_column
            for i in range(OWN):
                denom = (occ_at[0, oo * OWN + i] + occ_row[...]) - vir_pair
                inverse[a * ORB : (a + 1) * ORB, i * ORB : (i + 1) * ORB] = 1.0 / denom

    invert(range(0, 6))

    got(int_got.at[pl.ds(0, GROUP - 1)], pair_recv.at[8])

    for step in near:
        got(amp_z.at[around(z_hi, step)], pair_recv.at[-step % RING])
    put_rows(swap_order(take_rows(amp_z)), amp_cut_x)
    for step in far_first:
        send_pair(1, amp_cut_x.at[around(x, step)], amp_x.at[x], 4 + step % RING, at_x(step))
    amp_x[x] = amp_cut_x[x]
    join_from_partners([int_got[p] for p in range(GROUP)], turn.at[0], int_all.at[slot(1, oo)])
    spread_int(1)

    onward_direct()
    invert(range(6, 8))
    onward_int(0)
    relay_int(0, 0)

    for step in near:
        got(amp_x.at[around(x, step)], pair_recv.at[4 + -step % RING])
    join_from_partners(take_rows(amp_x), turn.at[1], amp_all.at[slot(1, vv)])
    spread_amp(1)
    relay_int(0, 1)
    relay_int(0, -1)
    relay_int(1, 0)
    onward_int(1, (1, -1))
    relay_int(0, 2)
    onward_int(1, (2,))
    pass_direct()
    onward_amp(1)
    def finish(kind):
        got(int_all.at[pl.ds(0, (8 if kind == 0 else 11) * CDS)], int_done.at[kind])
        got(amp_all.at[pl.ds(0, 8 * CDS)], amp_done.at[kind])

    finish(0)
    for at in range(0, WIDE, ROWS):
        partial[at : at + ROWS] = lax.dot_general(
            int_all[:CD, at : at + ROWS], amp_all[:CD], (((0,), (0,)), ((), ())),
            preferred_element_type=jnp.float32,
        )
    finish(1)
    got(amp_cut.at[pl.ds(0, RING - 1)], pair_send.at[0])
    got(amp_cut_x.at[pl.ds(0, RING - 1)], pair_send.at[1])
    got(int_cut.at[pl.ds(0, GROUP - 1)], pair_send.at[2])
    got(int_all.at[pl.ds(0, used["int"] * CDS)], int_send.at[0])
    got(amp_all.at[pl.ds(0, used["amp"] * CDS)], amp_send.at[0])


def gathered(integrals_t, amplitudes, occ_row, vir_row):
    whole = pltpu.VMEM((2 * CD, WIDE), jnp.bfloat16)

    square = pltpu.VMEM((WIDE, WIDE), jnp.float32)

    def pieces(*shape):
        return pltpu.VMEM((*shape, OWN, ORB), jnp.float32)

    blocks = pltpu.VMEM((RING, RING * OWN, ORB), jnp.bfloat16)

    def dma(*shape):
        return pltpu.SemaphoreType.DMA(shape)

    held = [pltpu.with_memory_space_constraint(a, pltpu.HBM) for a in (integrals_t, amplitudes, occ_row, vir_row)]
    return pl.pallas_call(
        gather_kernel,
        out_shape=(whole, whole, square, square),
        in_specs=[pl.BlockSpec(memory_space=pltpu.HBM)] * 4,
        out_specs=(pl.BlockSpec(memory_space=pltpu.VMEM),) * 4,
        scratch_shapes=[
            pieces(GROUP), pieces(GROUP), blocks, blocks, blocks, blocks,
            pltpu.VMEM((2, ORB, ORB), jnp.float32),
            pltpu.VMEM((1, ORB), jnp.float32), pltpu.VMEM((1, ORB), jnp.float32),
            pltpu.SMEM((1, ORB), jnp.float32), pltpu.SMEM((1, ORB), jnp.float32),
            dma(6), dma(3), dma(9), dma(1), dma(2, GROUP), dma(2), dma(1), dma(2, GROUP), dma(2),
        ],
        compiler_params=pltpu.CompilerParams(
            collective_id=0, has_side_effects=True, vmem_limit_bytes=32 << 20
        ),
        name="gather_pairs",
    )(*held)


def ladder_kernel(int_ref, amp_ref, inverse, partial, out_ref, made, sems):
    copies = []
    for s in range(WIDE // ROWS):
        rows = pl.ds(s * ROWS, ROWS)
        total = lax.dot_general(
            int_ref[CD:, s * ROWS : (s + 1) * ROWS], amp_ref[CD:], (((0,), (0,)), ((), ())),
            preferred_element_type=jnp.float32,
        )
        made[rows, :] = ((partial[rows, :] + total) * inverse[rows, :]).astype(made.dtype)
        copies.append(pltpu.make_async_copy(made.at[rows], out_ref.at[rows], sems.at[s]))
        copies[-1].start()
    for copy in copies:
        copy.wait()


def ladder(int_all, amp_all, inverse, partial):
    return pl.pallas_call(
        ladder_kernel,
        out_shape=jax.ShapeDtypeStruct((WIDE, WIDE), jnp.bfloat16),
        in_specs=[pl.BlockSpec(memory_space=pltpu.VMEM)] * 4,
        out_specs=pl.BlockSpec(memory_space=pl.ANY),
        scratch_shapes=[
            pltpu.VMEM((WIDE, WIDE), jnp.bfloat16), pltpu.SemaphoreType.DMA((WIDE // ROWS,)),
        ],
        compiler_params=pltpu.CompilerParams(vmem_limit_bytes=32 << 20),
        name="ladder_sum",
    )(int_all, amp_all, inverse, partial)


def on_device(integrals, amplitudes, occ_energy, vir_energy):
    return ladder(
        *gathered(integrals.T, amplitudes, occ_energy.reshape(1, ORB), vir_energy.reshape(1, ORB))
    )


def solution(mesh):
    placed = (P("vv", "oo"), P("vv", "oo"), P(), P())
    return jax.shard_map(
        on_device, mesh=mesh, in_specs=placed, out_specs=P("vv", "oo"), check_vma=False
    )
```

```python
import jax
import jax.numpy as jnp
from jax import lax
from jax.experimental import pallas as pl
from jax.experimental.pallas import tpu as pltpu
from jax.sharding import PartitionSpec as P

MESH = pl.DeviceIdType.MESH
GROUP = 16
CDS = 16
OWN = 8
ORB = 128
WIDE = OWN * ORB
CD = GROUP * CDS
RING = 4
ROWS = 256


def around(at, step):
    return (at + step + RING) % RING


def slot(kind, owner):
    return pl.ds(pl.multiple_of(kind * CD + owner * CDS, CDS), CDS)


def split_by_partner(chunk, turn):
    for j in range(OWN):
        turn[pl.ds(j, CDS, stride=OWN), :] = chunk[:, j * ORB : (j + 1) * ORB].astype(jnp.float32)
    turned = turn[...].T
    return [turned[p * OWN : (p + 1) * OWN] for p in range(GROUP)]


def swap_order(rows):
    return [rows[(p % RING) * RING + p // RING] for p in range(GROUP)]


def put_rows(rows, held):
    for q in range(RING):
        held[q] = jnp.concatenate(rows[q * RING : (q + 1) * RING], axis=0).astype(held.dtype)


def take_rows(held):
    blocks = [held[q].astype(jnp.float32) for q in range(RING)]
    return [blocks[p // RING][(p % RING) * OWN : (p % RING + 1) * OWN] for p in range(GROUP)]


def join_from_partners(rows, turn, chunk):
    group = lax.broadcasted_iota(jnp.int32, (OWN, ORB), 1) // OWN
    for bit in (1, 2, 4, 8):
        high = (group & bit) != 0
        for low in range(GROUP):
            if low & bit == 0:
                first, second = rows[low], rows[low + bit]
                rows[low] = jnp.where(high, pltpu.roll(second, bit * OWN, 1), first)
                rows[low + bit] = jnp.where(high, second, pltpu.roll(first, ORB - bit * OWN, 1))
    for c in range(CDS):
        turn[c * OWN : (c + 1) * OWN, :] = rows[c]
    for i in range(OWN):
        chunk[:, i * ORB : (i + 1) * ORB] = turn[pl.ds(i, CDS, stride=OWN), :].astype(chunk.dtype)


def gather_kernel(
    int_in, amp_in, occ_in, vir_in, int_all, amp_all, inverse, partial,
    int_cut, int_got, amp_cut, amp_z, amp_cut_x, amp_x, turn,
    occ_row, vir_row, occ_at, vir_at,
    local_sem, pair_send, pair_recv, int_send, int_recv, int_done, amp_send, amp_recv, amp_done,
):
    vv, oo = lax.axis_index("vv"), lax.axis_index("oo")
    y, z_lo, core = vv // 4, (vv // 2) % 2, vv % 2
    x, z_hi = oo // 4, oo % 4

    def at_y(step):
        return (around(y, step) * 4 + z_lo * 2 + core, oo)

    def at_x(step):
        return (vv, around(x, step) * 4 + z_hi)

    def at_z(step):
        return (vv, x * 4 + around(z_hi, step))

    def at_chip(y_step, other):
        return (around(y, y_step) * 4 + (1 - z_lo if other else z_lo) * 2 + core, oo)

    def at_vv(y_step, other, twin):
        return around(y, y_step) * 4 + (1 - z_lo if other else z_lo) * 2 + (1 - core if twin else core)

    sibling = (y * 4 + z_lo * 2 + 1 - core, oo)
    near, far_first = (1, -1, 2), (2, 1, -1)
    rows_of = [
        (y_step, other, twin)
        for y_step in (*far_first, 0) for other in (True, False) for twin in (True, False)
    ][:-1]
    chips = [
        (1, False), (-1, False), (0, True), (2, False), (1, True), (-1, True), (2, True)
    ]

    barrier = pltpu.get_barrier_semaphore()
    greeted = [at_z(step) for step in far_first] + [(at_vv(*steps), oo) for steps in rows_of] + [at_x(step) for step in far_first]
    loads = [
        pltpu.make_async_copy(int_in, int_all.at[slot(0, oo)], local_sem.at[0]),
        pltpu.make_async_copy(amp_in, amp_all.at[slot(0, vv)], local_sem.at[1]),
        pltpu.make_async_copy(occ_in, occ_row, local_sem.at[2]),
        pltpu.make_async_copy(vir_in, vir_row, local_sem.at[3]),
        pltpu.make_async_copy(occ_in, occ_at, local_sem.at[4]),
        pltpu.make_async_copy(vir_in, vir_at, local_sem.at[5]),
    ]
    for n, device in enumerate(greeted):
        if n in (1, 2):
            loads[2 - n].start()
        pl.semaphore_signal(barrier, inc=1, device_id=device, device_id_type=MESH)
    for load in loads[2:]:
        load.start()

    loads[1].wait()
    put_rows(swap_order(split_by_partner(amp_all.at[slot(0, vv)], turn.at[1])), amp_cut)
    loads[0].wait()
    for p, row in enumerate(split_by_partner(int_all.at[slot(0, oo)], turn.at[0])):
        int_cut[p] = row
    pl.semaphore_wait(barrier, len(greeted))

    def send(src, dst, send_sem, recv_sem, device):
        copy = pltpu.make_async_remote_copy(
            src_ref=src, dst_ref=dst, send_sem=send_sem, recv_sem=recv_sem,
            device_id=device, device_id_type=MESH,
        )
        copy.start()

    used = {"int": 0, "amp": 0}

    def send_int(kind, owner, device, last=False):
        rows = int_all.at[slot(kind, owner)]
        used["int"] += 1
        arrival = int_done.at[kind] if last else int_recv.at[kind, owner]
        send(rows, rows, int_send.at[0], arrival, device)

    def send_amp(kind, owner, device, last=False):
        rows = amp_all.at[slot(kind, owner)]
        used["amp"] += 1
        arrival = amp_done.at[kind] if last else amp_recv.at[kind, owner]
        send(rows, rows, amp_send.at[0], arrival, device)

    def send_pair(which, src, dst, arrival, device):
        send(src, dst, pair_send.at[which], pair_recv.at[arrival], device)

    def got(ref, sem):
        pltpu.make_async_copy(ref, ref, sem).wait()

    def got_int(kind, owner):
        got(int_all.at[slot(kind, owner)], int_recv.at[kind, owner])

    def got_amp(kind, owner):
        got(amp_all.at[slot(kind, owner)], amp_recv.at[kind, owner])

    def spread_int(kind):
        for step in far_first:
            send_int(kind, oo, at_z(step))
        for step in (1, -1) if kind == 0 else far_first:
            send_int(kind, oo, at_x(step), last=step == -1 or (kind == 1 and step == 1))

    def spread_amp(kind):
        for step, other in chips[::-1]:
            send_amp(kind, vv, at_chip(step, other))
        send_amp(kind, vv, sibling, last=True)

    def owner_int(x_step, z_step):
        return around(x, x_step) * 4 + around(z_hi, z_step)

    def owner_amp(y_step, other):
        return around(y, y_step) * 4 + (1 - z_lo if other else z_lo) * 2 + core

    def onward_int(kind, z_steps=near):
        for z_step in z_steps:
            got_int(kind, owner_int(0, z_step))
            relayed = kind == 0 and z_step != 2
            for step in far_first if z_step == 2 else (1, -1):
                last = not relayed or step != (1 if z_step % 2 == 0 else -1)
                send_int(kind, owner_int(0, z_step), at_x(step), last)

    def corner_int():
        got_int(1, owner_int(2, 0))
        for step in (1, -1):
            send_int(1, owner_int(2, 0), at_z(step), last=True)

    def relay_int(kind, z_step):
        first = -1 if z_step % 2 == 0 else 1
        got_int(kind, owner_int(first, z_step))
        send_int(kind, owner_int(first, z_step), at_x(-first), last=True)

    def onward_amp(kind):
        for step, other in chips:
            got_amp(kind, owner_amp(step, other))
            send_amp(kind, owner_amp(step, other), sibling, last=True)

    def spread_direct():
        send_amp(0, vv, at_chip(0, True))
        for step in far_first:
            send_amp(0, vv, at_chip(step, False))
        send_amp(0, vv, sibling, last=True)

    def onward_direct():
        got_amp(0, owner_amp(0, True))
        for step in far_first:
            send_amp(0, owner_amp(0, True), at_chip(step, False))
        send_amp(0, owner_amp(0, True), sibling, last=True)

    def pass_direct():
        for other in (False, True):
            for step in near:
                got_amp(0, owner_amp(step, other))
                send_amp(0, owner_amp(step, other), sibling, last=True)

    for step in far_first:
        send_pair(0, amp_cut.at[around(z_hi, step)], amp_z.at[z_hi], 0, at_z(step))
    for steps in rows_of:
        partner = at_vv(*steps)
        send_pair(2, int_cut.at[partner], int_got.at[vv], 8, (partner, oo))
    amp_z[z_hi] = amp_cut[z_hi]
    int_got[vv] = int_cut[vv]
    spread_int(0)
    spread_direct()
    for load in loads[2:]:
        load.wait()
    vir_column = jnp.broadcast_to(vir_row[...], (ORB, ORB)).T

    def invert(blocks):
        for a in blocks:
            vir_pair = vir_at[0, vv * OWN + a] + vir_column
            for i in range(OWN):
                denom = (occ_at[0, oo * OWN + i] + occ_row[...]) - vir_pair
                inverse[a * ORB : (a + 1) * ORB, i * ORB : (i + 1) * ORB] = 1.0 / denom

    invert(range(0, 6))

    got(int_got.at[pl.ds(0, GROUP - 1)], pair_recv.at[8])

    got(amp_z.at[pl.ds(0, RING - 1)], pair_recv.at[0])
    put_rows(swap_order(take_rows(amp_z)), amp_cut_x)
    for step in far_first:
        send_pair(1, amp_cut_x.at[around(x, step)], amp_x.at[x], 4, at_x(step))
    amp_x[x] = amp_cut_x[x]
    join_from_partners([int_got[p] for p in range(GROUP)], turn.at[0], int_all.at[slot(1, oo)])
    spread_int(1)

    onward_direct()
    invert(range(6, 8))
    onward_int(0)
    relay_int(0, 0)

    got(amp_x.at[pl.ds(0, RING - 1)], pair_recv.at[4])
    join_from_partners(take_rows(amp_x), turn.at[1], amp_all.at[slot(1, vv)])
    spread_amp(1)
    relay_int(0, 1)
    relay_int(0, -1)
    onward_int(1, (1, -1))
    onward_int(1, (2,))
    corner_int()
    pass_direct()
    onward_amp(1)
    def finish(kind):
        got(int_all.at[pl.ds(0, (9 if kind == 0 else 11) * CDS)], int_done.at[kind])
        got(amp_all.at[pl.ds(0, 8 * CDS)], amp_done.at[kind])

    finish(0)
    for at in range(0, WIDE, ROWS):
        partial[at : at + ROWS] = lax.dot_general(
            int_all[:CD, at : at + ROWS], amp_all[:CD], (((0,), (0,)), ((), ())),
            preferred_element_type=jnp.float32,
        )
    finish(1)
    got(amp_cut.at[pl.ds(0, RING - 1)], pair_send.at[0])
    got(amp_cut_x.at[pl.ds(0, RING - 1)], pair_send.at[1])
    got(int_cut.at[pl.ds(0, GROUP - 1)], pair_send.at[2])
    got(int_all.at[pl.ds(0, used["int"] * CDS)], int_send.at[0])
    got(amp_all.at[pl.ds(0, used["amp"] * CDS)], amp_send.at[0])


def gathered(integrals_t, amplitudes, occ_row, vir_row):
    whole = pltpu.VMEM((2 * CD, WIDE), jnp.bfloat16)

    square = pltpu.VMEM((WIDE, WIDE), jnp.float32)

    def pieces(*shape):
        return pltpu.VMEM((*shape, OWN, ORB), jnp.float32)

    blocks = pltpu.VMEM((RING, RING * OWN, ORB), jnp.bfloat16)

    def dma(*shape):
        return pltpu.SemaphoreType.DMA(shape)

    held = [pltpu.with_memory_space_constraint(a, pltpu.HBM) for a in (integrals_t, amplitudes, occ_row, vir_row)]
    return pl.pallas_call(
        gather_kernel,
        out_shape=(whole, whole, square, square),
        in_specs=[pl.BlockSpec(memory_space=pltpu.HBM)] * 4,
        out_specs=(pl.BlockSpec(memory_space=pltpu.VMEM),) * 4,
        scratch_shapes=[
            pieces(GROUP), pieces(GROUP), blocks, blocks, blocks, blocks,
            pltpu.VMEM((2, ORB, ORB), jnp.float32),
            pltpu.VMEM((1, ORB), jnp.float32), pltpu.VMEM((1, ORB), jnp.float32),
            pltpu.SMEM((1, ORB), jnp.float32), pltpu.SMEM((1, ORB), jnp.float32),
            dma(6), dma(3), dma(9), dma(1), dma(2, GROUP), dma(2), dma(1), dma(2, GROUP), dma(2),
        ],
        compiler_params=pltpu.CompilerParams(
            collective_id=0, has_side_effects=True, vmem_limit_bytes=32 << 20
        ),
        name="gather_pairs",
    )(*held)


def ladder_kernel(int_ref, amp_ref, inverse, partial, out_ref, made, sems):
    copies = []
    for s in range(WIDE // ROWS):
        rows = pl.ds(s * ROWS, ROWS)
        total = lax.dot_general(
            int_ref[CD:, s * ROWS : (s + 1) * ROWS], amp_ref[CD:], (((0,), (0,)), ((), ())),
            preferred_element_type=jnp.float32,
        )
        made[rows, :] = ((partial[rows, :] + total) * inverse[rows, :]).astype(made.dtype)
        copies.append(pltpu.make_async_copy(made.at[rows], out_ref.at[rows], sems.at[s]))
        copies[-1].start()
    for copy in copies:
        copy.wait()


def ladder(int_all, amp_all, inverse, partial):
    return pl.pallas_call(
        ladder_kernel,
        out_shape=jax.ShapeDtypeStruct((WIDE, WIDE), jnp.bfloat16),
        in_specs=[pl.BlockSpec(memory_space=pltpu.VMEM)] * 4,
        out_specs=pl.BlockSpec(memory_space=pl.ANY),
        scratch_shapes=[
            pltpu.VMEM((WIDE, WIDE), jnp.bfloat16), pltpu.SemaphoreType.DMA((WIDE // ROWS,)),
        ],
        compiler_params=pltpu.CompilerParams(vmem_limit_bytes=32 << 20),
        name="ladder_sum",
    )(int_all, amp_all, inverse, partial)


def on_device(integrals, amplitudes, occ_energy, vir_energy):
    return ladder(
        *gathered(integrals.T, amplitudes, occ_energy.reshape(1, ORB), vir_energy.reshape(1, ORB))
    )


def solution(mesh):
    placed = (P("vv", "oo"), P("vv", "oo"), P(), P())
    return jax.shard_map(
        on_device, mesh=mesh, in_specs=placed, out_specs=P("vv", "oo"), check_vma=False
    )
```
